128 devices in a mesh: aa: 8 (over y_lo, z), ba: 16 (over y_hi, x, core).
Axes of the slice: x: 4, y: 4 (y_hi: 2, y_lo: 2; y = y_hi * 2 + y_lo), z: 4, core: 2. Of those that a mesh axis runs over, the one named last changes fastest.
Arguments:
- atom_cond: float32 [24576, 128], P(('aa', 'ba')), may hold values from -6 to 6
- noisy_pos: float32 [3, 24576], P(None, ('aa', 'ba')), may hold values from -8 to 8
- noise_level: float32 [1], replicated, may hold values from 0.1 to 4
- atom_token: int32 [24576], P(('aa', 'ba')), may hold values from -1 to 2047, as said below
- token_cond: float32 [2048, 768], P('aa'), may hold values from -6 to 6
- pair: bfloat16 [2048, 2048, 128], P('aa', 'ba'), may hold values from -64 to 64
- pair_bias_weight: bfloat16 [16, 128], replicated, may hold values from -0.375 to 0.375
- gains: float32 [3, 768], replicated, may hold values from 0.25 to 1.75
- w_pos: float32 [3, 128], replicated, may hold values from -3.5 to 3.5
- w_atom_token: bfloat16 [128, 768], replicated, may hold values from -0.5 to 0.5
- w_query_gate: bfloat16 [768, 1536], replicated, may hold values from -0.21875 to 0.21875
- w_key_value: bfloat16 [768, 1536], replicated, may hold values from -0.21875 to 0.21875
- w_attn_out: bfloat16 [768, 768], replicated, may hold values from -0.21875 to 0.21875
- w_up: bfloat16 [768, 3072], replicated, may hold values from -0.21875 to 0.21875
- w_down: bfloat16 [1536, 768], replicated, may hold values from -0.15625 to 0.15625
- w_token_atom: bfloat16 [768, 128], replicated, may hold values from -0.21875 to 0.21875
- w_pos_out: bfloat16 [3, 128], replicated, may hold values from -0.5 to 0.5
Outputs:
- denoised: float32 [3, 24576], P(None, ('aa', 'ba'))
- token_out: float32 [2048, 768], P('aa')
The draws below stay inside these ranges and needn't reach their ends.
Inputs may be any that keep to these rules, and one draw needn't show every extreme that they name: `atom_token`: atom slots come in 8 groups of 3072 consecutive slots; group r holds only atoms of tokens r * 256 to (r + 1) * 256 - 1, in nondecreasing token order, live slots first and -1 after them. Every token has 1 to 12 atoms, and some token of every group has exactly 12.
All inputs are finite; a program needn't handle non-finite values.
Results may differ from the reference program's by a relative error of at most 0.01.
Values may be sent and summed in bfloat16 or wider, within the bound.
No kernel may reach another device: no remote copies, remote signals or barrier semaphores. Data moves between devices by JAX's collectives and lax.ppermute only.
A program may use at most 128 MiB of HBM per device.

```python
import math
import jax
import jax.numpy as jnp
from jax import lax

D = 768
HEADS = 16
PAIR_C = 128
ATOM_C = 128
FF = 1536
TOK_A = 256
PER_TOKEN = 12
TOKENS = 2048
ATOMS = 24576
N_BA = 16


def bias_table(key):
    return 0.125 * jax.random.truncated_normal(jax.random.fold_in(key, 11), -3.0, 3.0, (HEADS, PAIR_C), jnp.float32)


def draw_pair_bias_weight(key, part):
    return bias_table(key).astype(jnp.bfloat16)


def draw_pair(key, part):
    base_key = jax.random.fold_in(key, 12)
    field = jax.random.truncated_normal(base_key, -6.0, 6.0, (TOKENS, TOKENS, PAIR_C), jnp.float32)
    table = bias_table(key).astype(jnp.bfloat16).astype(jnp.float32)
    pick_rows = jax.random.randint(jax.random.fold_in(key, 13), (HEADS, 3), 0, TOKENS)
    pick_cols = jax.random.randint(jax.random.fold_in(key, 14), (HEADS, 3), 0, TOKENS)
    pick_steps = jax.random.randint(jax.random.fold_in(key, 15), (HEADS, 3), 1, TOKENS)
    for head_index in range(HEADS):
        sign_row = jnp.sign(table[head_index])
        weight_total = jnp.maximum(jnp.sum(jnp.abs(table[head_index])), 0.5)
        for level_index, strength in enumerate((120.0, 180.0, 240.0)):
            row_pick = pick_rows[head_index, level_index]
            first_col = pick_cols[head_index, level_index]
            second_col = (first_col + pick_steps[head_index, level_index]) % TOKENS
            field = field.at[row_pick, first_col].set(strength / weight_total * sign_row)
            field = field.at[row_pick, second_col].set((strength - 2.0) / weight_total * sign_row)
    return field.astype(jnp.bfloat16)


def draw_atom_token(key, part):
    groups = TOKENS // TOK_A
    upper_count = jax.random.randint(jax.random.fold_in(key, 21), (groups, 1), PER_TOKEN // 2, PER_TOKEN + 1)
    raw_bits = jax.random.randint(jax.random.fold_in(key, 22), (groups, TOK_A), 0, 1 << 20)
    counts = 1 + raw_bits % upper_count
    chosen = jax.random.randint(jax.random.fold_in(key, 23), (groups, 1), 0, TOK_A)
    counts = jnp.where(jnp.arange(TOK_A, dtype=jnp.int32)[None, :] == chosen, PER_TOKEN, counts)
    ends = jnp.cumsum(counts, axis=1)
    slots = jnp.arange(PER_TOKEN * TOK_A, dtype=jnp.int32)
    owner = jnp.sum((ends[:, None, :] <= slots[None, :, None]).astype(jnp.int32), axis=2)
    token_ids = owner + (jnp.arange(groups, dtype=jnp.int32) * TOK_A)[:, None]
    return jnp.where(owner < TOK_A, token_ids, -1).reshape(-1).astype(jnp.int32)


def level_of(stream_key, dims, cuts, low, high):
    factor_of = 1.0
    for dim, parts in cuts:
        draws = jax.random.uniform(jax.random.fold_in(jax.random.fold_in(stream_key, 6), dim), (parts,), jnp.float32, low / len(cuts), high / len(cuts))
        factor_of = factor_of * jnp.repeat(jnp.exp(draws), dims[dim] // parts).reshape((-1,) + (1,) * (len(dims) - 1 - dim))
    return factor_of


def centred(stream_key, shape, width, reach, shards=(), held_as=jnp.bfloat16):
    factor_of = level_of(stream_key, shape, shards, -0.22, 0.18) if shards else 1.0
    entries = jax.random.normal(stream_key, shape, jnp.float32) * width * factor_of
    return jnp.minimum(jnp.maximum(entries, -reach), reach).astype(held_as)


def setup_inputs(seed: int = 0) -> dict:
    streams_of = jax.random.split(jax.random.key(seed), 18)
    return {
        "atom_cond": centred(streams_of[0], (ATOMS, ATOM_C), 1.0, 6.0, ((0, 128),), jnp.float32),
        "noisy_pos": centred(streams_of[1], (3, ATOMS), 1.5, 8.0, ((1, 128),), jnp.float32),
        "noise_level": jnp.clip(jnp.exp(jax.random.uniform(streams_of[2], (1,), jnp.float32, math.log(0.1), math.log(4.0))), 0.1, 4.0),
        "atom_token": draw_atom_token(jax.random.fold_in(streams_of[17], 71), 0),
        "token_cond": centred(streams_of[4], (TOKENS, D), 1.0, 6.0, ((0, 8),), jnp.float32),
        "pair": draw_pair(jax.random.fold_in(streams_of[17], 71), 0),
        "pair_bias_weight": draw_pair_bias_weight(jax.random.fold_in(streams_of[17], 71), 0),
        "gains": jnp.clip(1.0 + 0.15 * jax.random.normal(streams_of[7], (3, D), jnp.float32), 0.25, 1.75),
        "w_pos": centred(streams_of[8], (3, ATOM_C), 3 ** -0.5, 3.5, (), jnp.float32),
        "w_atom_token": centred(streams_of[9], (ATOM_C, D), ATOM_C ** -0.5, 0.5),
        "w_query_gate": centred(streams_of[10], (D, 2 * D), D ** -0.5, 0.21875),
        "w_key_value": centred(streams_of[11], (D, 2 * D), D ** -0.5, 0.21875),
        "w_attn_out": centred(streams_of[12], (D, D), D ** -0.5, 0.21875),
        "w_up": centred(streams_of[13], (D, 2 * FF), D ** -0.5, 0.21875),
        "w_down": centred(streams_of[14], (FF, D), FF ** -0.5, 0.15625),
        "w_token_atom": centred(streams_of[15], (D, ATOM_C), D ** -0.5, 0.21875),
        "w_pos_out": centred(streams_of[16], (3, ATOM_C), ATOM_C ** -0.5, 0.5),
    }


def layer_norm(values, gain_row):
    mean_value = lax.optimization_barrier(jnp.mean(values, axis=-1, keepdims=True))
    centered = values - mean_value
    variance = lax.optimization_barrier(jnp.mean(centered * centered, axis=-1, keepdims=True))
    return centered * lax.rsqrt(variance + 1e-05) * gain_row

def reference(atom_cond, noisy_pos, noise_level, atom_token, token_cond, pair, pair_bias_weight, gains, w_pos, w_atom_token, w_query_gate, w_key_value, w_attn_out, w_up, w_down, w_token_atom, w_pos_out):
    noise_sigma = noise_level[0]
    inv_scale = 1.0 / jnp.sqrt(noise_sigma * noise_sigma + 1.0)
    scaled_pos = noisy_pos * inv_scale
    atom_state = atom_cond + scaled_pos[0][:, None] * w_pos[0]
    atom_state = atom_state + scaled_pos[1][:, None] * w_pos[1]
    atom_state = atom_state + scaled_pos[2][:, None] * w_pos[2]
    hidden_atom = jax.nn.relu(jnp.dot(atom_state.astype(jnp.bfloat16), w_atom_token, preferred_element_type=jnp.float32)).astype(jnp.bfloat16)
    live_mask = atom_token >= 0
    segment_ids = jnp.where(live_mask, atom_token, TOKENS).astype(jnp.int32)
    summed = jax.ops.segment_sum(hidden_atom.astype(jnp.float32), segment_ids, num_segments=TOKENS + 1)[:TOKENS]
    counts = jax.ops.segment_sum(live_mask.astype(jnp.float32), segment_ids, num_segments=TOKENS + 1)[:TOKENS]
    tokens_start = token_cond + summed / counts[:, None]
    normed = layer_norm(tokens_start, gains[0]).astype(jnp.bfloat16)
    query_gate = jnp.dot(normed, w_query_gate, preferred_element_type=jnp.float32)
    query_rows = query_gate[:, :D].astype(jnp.bfloat16)
    gate_value = jax.nn.sigmoid(query_gate[:, D:]).astype(jnp.bfloat16)
    key_value = jnp.dot(normed, w_key_value, preferred_element_type=jnp.float32).astype(jnp.bfloat16)
    head_dim = D // HEADS
    block_cols = TOKENS // N_BA
    query_heads = query_rows.astype(jnp.float32).reshape(TOKENS, HEADS, head_dim)
    bias_weight = pair_bias_weight.astype(jnp.float32)

    def one_block(block_index):
        start_row = block_index * block_cols
        kv_block = lax.dynamic_slice_in_dim(key_value, start_row, block_cols, 0).astype(jnp.float32)
        key_heads = kv_block[:, :D].reshape(block_cols, HEADS, head_dim)
        value_heads = kv_block[:, D:].reshape(block_cols, HEADS, head_dim)
        pair_block = lax.dynamic_slice_in_dim(pair, start_row, block_cols, 1).astype(jnp.float32)
        scores = jnp.einsum('ihd,jhd->hij', query_heads, key_heads) * head_dim ** (-0.5) + jnp.einsum('hc,ijc->hij', bias_weight, pair_block)
        block_max = lax.optimization_barrier(jnp.max(scores, axis=2))
        weights = jnp.exp(scores - block_max[:, :, None])
        block_total = lax.optimization_barrier(jnp.sum(weights, axis=2))
        rounded = lax.optimization_barrier(weights.astype(jnp.bfloat16)).astype(jnp.float32)
        partial_out = jnp.einsum('hij,jhd->ihd', rounded, value_heads).reshape(TOKENS, D)
        return (block_max, block_total, partial_out)
    maxima, totals, outputs = lax.map(one_block, jnp.arange(N_BA, dtype=jnp.int32))
    overall = lax.optimization_barrier(jnp.max(maxima, axis=0))
    factors = jnp.exp(maxima - overall[None])
    total_all = lax.optimization_barrier(jnp.sum(factors * totals, axis=0))
    widened = jnp.repeat(jnp.transpose(factors, (0, 2, 1)), head_dim, axis=2)
    out_all = lax.optimization_barrier(jnp.sum(widened * outputs, axis=0))
    attended = out_all / jnp.repeat(total_all.T, head_dim, axis=1)
    mixed_heads = (attended * gate_value.astype(jnp.float32)).astype(jnp.bfloat16)
    tokens_mid = tokens_start + jnp.dot(mixed_heads, w_attn_out, preferred_element_type=jnp.float32)
    normed_mid = layer_norm(tokens_mid, gains[1]).astype(jnp.bfloat16)
    gate_up = jnp.dot(normed_mid, w_up, preferred_element_type=jnp.float32)
    inner_units = (jax.nn.silu(gate_up[:, :FF]) * gate_up[:, FF:]).astype(jnp.bfloat16)
    token_out = tokens_mid + jnp.dot(inner_units, w_down, preferred_element_type=jnp.float32)
    normed_out = layer_norm(token_out, gains[2]).astype(jnp.bfloat16)
    token_atom = jnp.dot(normed_out, w_token_atom, preferred_element_type=jnp.float32).astype(jnp.bfloat16)
    safe_ids = jnp.clip(atom_token, 0, TOKENS - 1).astype(jnp.int32)
    picked = jnp.where(live_mask[:, None], token_atom[safe_ids].astype(jnp.float32), 0.0)
    atom_final = atom_state + picked
    atom_normed = layer_norm(atom_final, 1.0).astype(jnp.bfloat16)
    update = lax.dot_general(w_pos_out, atom_normed, (((1,), (1,)), ((), ())), preferred_element_type=jnp.float32)
    denoised = noisy_pos * (inv_scale * inv_scale) + update * (noise_sigma * inv_scale)
    return (denoised, token_out)
```

```python
import functools

import jax
import jax.numpy as jnp
from jax import lax
from jax.experimental import pallas as pl
from jax.experimental.pallas import tpu as pltpu
from jax.sharding import PartitionSpec as P

D = 768
HEADS = 16
HEAD_DIM = D // HEADS
BF = jnp.bfloat16
F32 = jnp.float32
WIDE = jnp.float16
MIB = 1 << 20


def dot(a, b, dims=((1,), (0,)), **kw):
    return lax.dot_general(a, b, (dims, ((), ())), preferred_element_type=F32, **kw)


def norm_rows(values, gain_row):
    mean_value = jnp.mean(values, axis=-1, keepdims=True)
    centered = values - mean_value
    variance = jnp.mean(centered * centered, axis=-1, keepdims=True)
    return centered * lax.rsqrt(variance + 1e-05) * gain_row


def whole(n):
    return [pl.BlockSpec(memory_space=pltpu.VMEM)] * n


def state_kernel(cond_ref, pos_ref, noise_ref, ids_ref, w_pos_ref, state_ref, packed_ref):
    atoms = cond_ref.shape[0]
    sigma = noise_ref[0]
    sigma = jnp.full((1, 128), sigma, F32)
    inv = 1.0 / jnp.sqrt(sigma * sigma + 1.0)
    pos = jnp.transpose(
        jnp.concatenate([pos_ref[...] * inv[:, :1], jnp.zeros((5, atoms), F32)], axis=0)
    )
    state = cond_ref[...] + pos[:, 0:1] * w_pos_ref[0:1, :]
    state = state + pos[:, 1:2] * w_pos_ref[1:2, :]
    state = state + pos[:, 2:3] * w_pos_ref[2:3, :]
    state_ref[...] = state
    ids = ids_ref[...].astype(F32)
    first = ids[:, :128]
    second = jnp.concatenate([ids[:, 128:], jnp.zeros((1, 256 - atoms), F32)], axis=1)
    tail = jnp.concatenate([first, second, jnp.zeros((14, 128), F32)], axis=0).astype(BF)
    rounded = state.astype(BF)
    for piece in range(packed_ref.shape[0]):
        packed_ref[piece, :atoms, :] = rounded
        packed_ref[piece, atoms:, :] = tail


def bias_kernel(pair_ref, w_ref, out_ref, held):
    rows, cols, chans = pair_ref.shape
    half = rows // 2
    both = jnp.concatenate(
        [
            pair_ref[:half].reshape(half * cols, chans),
            pair_ref[half:].reshape(half * cols, chans),
        ],
        axis=1,
    )
    bias = dot(w_ref[...], both, ((1,), (1,)))
    for i in range(half):
        held[pl.ds(i, HEADS, stride=rows), :] = bias[:HEADS, i * cols : (i + 1) * cols]
        held[pl.ds(half + i, HEADS, stride=rows), :] = bias[HEADS:, i * cols : (i + 1) * cols]
    out_ref[...] = held[...].reshape(HEADS, rows, cols).astype(out_ref.dtype)


def token_kernel(
    mine_ref, other_ref, w_atom_ref, cond_ref, gains_ref, w_head_ref,
    start_ref, query_ref, gate_ref, kv_ref,
):
    tok_rows = cond_ref.shape[0]
    atoms = mine_ref.shape[1] - 16
    tokens = lax.broadcasted_iota(jnp.int32, (tok_rows, atoms), 0).astype(F32)
    sums = jnp.zeros((tok_rows, D), F32)
    counts = jnp.zeros((tok_rows, atoms), F32)
    for ref in (mine_ref, other_ref):
        for piece in range(ref.shape[0]):
            hidden = jax.nn.relu(dot(ref[piece, :atoms, :], w_atom_ref[...])).astype(BF)
            tail = ref[piece, atoms:, :].astype(F32)
            ids = jnp.concatenate([tail[0:1, :], tail[1:2, : atoms - 128]], axis=1)
            chosen = jnp.where(ids == tokens, 1.0, 0.0)
            counts += chosen
            sums += dot(chosen.astype(BF), hidden)
    start = cond_ref[...] + sums / jnp.sum(counts, axis=1, keepdims=True)
    start_ref[...] = start
    normed = norm_rows(start, gains_ref[0:1, :]).astype(BF)
    projected = dot(normed, w_head_ref[...])
    query_ref[...] = projected[:, :HEAD_DIM].astype(BF)
    gate_ref[...] = jax.nn.sigmoid(projected[:, 128 : 128 + HEAD_DIM]).astype(BF)
    kv = jnp.transpose(projected[:, 256:512])
    kv = jnp.concatenate([kv[:HEAD_DIM], kv[128 : 128 + HEAD_DIM]], axis=0).astype(BF)
    for piece in range(kv_ref.shape[0]):
        kv_ref[piece] = kv


def attend_kernel(query_ref, gate_ref, kv_ref, bias_ref, mixed_ref):
    groups, _, keys = kv_ref.shape
    tok_rows = query_ref.shape[0]
    blocks, _, cols = bias_ref.shape
    step = 64
    parts = []
    for r in range(0, tok_rows, step):
        query = query_ref[r : r + step, :]
        scores = jnp.concatenate(
            [dot(query, kv_ref[g, :HEAD_DIM, :]) for g in range(groups)], axis=1
        ) * HEAD_DIM ** (-0.5)
        bias = jnp.concatenate(
            [bias_ref[b, r : r + step, :].astype(F32) for b in range(blocks)], axis=1
        )
        scores = scores + bias
        top = jnp.max(scores, axis=1, keepdims=True)
        weights = jnp.exp(scores - top)
        total = jnp.sum(weights, axis=1, keepdims=True)
        rounded = weights.astype(BF)
        out = jnp.zeros((step, HEAD_DIM), F32)
        for g in range(groups):
            out += dot(
                rounded[:, g * keys : (g + 1) * keys], kv_ref[g, HEAD_DIM:, :], ((1,), (1,))
            )
        parts.append(out / total)
    attended = jnp.concatenate(parts, axis=0)
    mixed = attended * gate_ref[...].astype(F32)
    mixed = jnp.concatenate([mixed, jnp.zeros((tok_rows, 128 - HEAD_DIM), F32)], axis=1)
    turned = jnp.transpose(mixed)[:HEAD_DIM].astype(BF)
    for piece in range(mixed_ref.shape[0]):
        mixed_ref[piece] = turned


def close_kernel(
    mine_ref, other_ref, w_out_ref, start_ref, gains_ref, w_up_ref, w_down_ref, w_tok_ref,
    state_ref, ids_ref, w_pos_ref, pos_ref, noise_ref,
    denoised_ref, token_ref,
):
    core = lax.rem(lax.axis_index("ba"), 2)
    tok_rows = start_ref.shape[0]
    pieces = mine_ref.shape[0]
    width = pieces * HEAD_DIM
    mine = mine_ref[...].reshape(width, tok_rows)
    other = other_ref[...].reshape(width, tok_rows)
    added = dot(mine, w_out_ref[:, core].reshape(width, D), ((0,), (0,)))
    added += dot(other, w_out_ref[:, 1 - core].reshape(width, D), ((0,), (0,)))
    mid = start_ref[...] + added
    normed = norm_rows(mid, gains_ref[1:2, :]).astype(BF)
    hidden = w_down_ref.shape[0]
    first = dot(normed, w_up_ref[:, :hidden])
    second = dot(normed, w_up_ref[:, hidden:])
    inner = (jax.nn.silu(first) * second).astype(BF)
    token_out = mid + dot(inner, w_down_ref[...])
    token_ref[...] = token_out
    normed = norm_rows(token_out, gains_ref[2:3, :]).astype(BF)
    token_atom = dot(normed, w_tok_ref[...]).astype(BF)
    atoms = state_ref.shape[0]
    tokens = lax.broadcasted_iota(jnp.int32, (tok_rows, atoms), 0)
    chosen = jnp.where(ids_ref[...] == tokens, 1.0, 0.0).astype(BF)
    final = state_ref[...] + dot(chosen, token_atom, ((0,), (0,)))
    normed = norm_rows(final, 1.0).astype(BF)
    update = dot(w_pos_ref[...], normed, ((1,), (1,)))
    sigma = jnp.full((1, 128), noise_ref[0], F32)
    inv = (1.0 / jnp.sqrt(sigma * sigma + 1.0))[:, :1]
    denoised_ref[...] = pos_ref[...] * (inv * inv) + update * (sigma[:, :1] * inv)


def shape(dims, dtype):
    return jax.ShapeDtypeStruct(dims, dtype)


def on_device(
    atom_cond, noisy_pos, noise_level, atom_token, token_cond, pair, pair_bias_weight, gains,
    w_pos, w_atom_token, w_query_gate, w_key_value, w_attn_out, w_up, w_down, w_token_atom,
    w_pos_out,
):
    atoms, chans = atom_cond.shape
    tok_rows = token_cond.shape[0]
    cols = pair.shape[1]
    size = lax.axis_size("ba")
    peers = size // 2
    groups = lax.axis_size("aa")
    row_index = lax.axis_index("aa")
    head = lax.axis_index("ba")
    same_core = [list(range(core, size, 2)) for core in range(2)]
    siblings = [(i, i ^ 1) for i in range(size)]
    smem = pl.BlockSpec(memory_space=pltpu.SMEM)

    def gathered(copies):
        mine = lax.all_to_all(copies, "ba", 0, 0, tiled=True, axis_index_groups=same_core)
        return mine, lax.ppermute(mine, "ba", siblings)

    local_ids = jnp.maximum(atom_token - row_index * tok_rows, -1)[None, :]
    state, packed = pl.pallas_call(
        state_kernel,
        out_shape=(shape((atoms, chans), F32), shape((peers, atoms + 16, chans), BF)),
        in_specs=[*whole(2), smem, *whole(2)],
        out_specs=tuple(whole(2)),
        name="state",
    )(atom_cond, noisy_pos, noise_level, local_ids, w_pos)

    block = 32
    zeros = jnp.zeros_like(pair_bias_weight)
    w_both = jnp.concatenate(
        [
            jnp.concatenate([pair_bias_weight, zeros], axis=1),
            jnp.concatenate([zeros, pair_bias_weight], axis=1),
        ],
        axis=0,
    )
    bias = pl.pallas_call(
        bias_kernel,
        grid=(tok_rows // block,),
        out_shape=shape((HEADS, tok_rows, cols), F32),
        in_specs=[
            pl.BlockSpec((block, cols, chans), lambda i: (i, 0, 0)),
            pl.BlockSpec(w_both.shape, lambda i: (0, 0)),
        ],
        out_specs=pl.BlockSpec((HEADS, block, cols), lambda i: (0, i, 0)),
        scratch_shapes=[pltpu.VMEM((HEADS * block, cols), F32)],
        compiler_params=pltpu.CompilerParams(vmem_limit_bytes=24 * MIB),
        cost_estimate=pl.CostEstimate(
            flops=2 * tok_rows * cols * chans * 256, bytes_accessed=pair.size * 2 + 2 * MIB,
            transcendentals=0,
        ),
        name="bias",
    )(pair, w_both)
    bias = lax.all_to_all(bias.astype(WIDE), "ba", 0, 0, tiled=True).astype(F32)

    def column(w, at):
        part = lax.dynamic_slice_in_dim(w, at, HEAD_DIM, 1)
        return jnp.pad(part, ((0, 0), (0, 128 - HEAD_DIM)))

    w_head = jnp.concatenate(
        [
            column(w_query_gate, head * HEAD_DIM),
            column(w_query_gate, D + head * HEAD_DIM),
            column(w_key_value, head * HEAD_DIM),
            column(w_key_value, D + head * HEAD_DIM),
        ],
        axis=1,
    )

    mine, other = gathered(packed)
    start, query, gate, kv = pl.pallas_call(
        token_kernel,
        out_shape=(
            shape((tok_rows, D), F32),
            shape((tok_rows, HEAD_DIM), BF),
            shape((tok_rows, HEAD_DIM), BF),
            shape((groups, 2 * HEAD_DIM, tok_rows), BF),
        ),
        in_specs=whole(6),
        out_specs=tuple(whole(4)),
        compiler_params=pltpu.CompilerParams(vmem_limit_bytes=32 * MIB),
        name="token",
    )(mine, other, w_atom_token, token_cond, gains, w_head)
    kv = lax.all_to_all(kv, "aa", 0, 0, tiled=True)

    mixed = pl.pallas_call(
        attend_kernel,
        out_shape=shape((peers, HEAD_DIM, tok_rows), BF),
        in_specs=whole(4),
        out_specs=whole(1)[0],
        compiler_params=pltpu.CompilerParams(vmem_limit_bytes=32 * MIB),
        name="attend",
    )(query, gate, kv, bias)
    mine, other = gathered(mixed)

    return pl.pallas_call(
        close_kernel,
        out_shape=(shape((3, atoms), F32), shape((tok_rows, D), F32)),
        in_specs=[*whole(12), smem],
        out_specs=tuple(whole(2)),
        compiler_params=pltpu.CompilerParams(vmem_limit_bytes=40 * MIB),
        name="close",
    )(
        mine, other, w_attn_out.reshape(peers, 2, HEAD_DIM, D), start, gains, w_up, w_down,
        w_token_atom, state, local_ids, w_pos_out, noisy_pos, noise_level,
    )


def solution(mesh):
    both = ("aa", "ba")
    in_specs = (
        P(both, None), P(None, both), P(), P(both), P("aa", None), P("aa", "ba", None),
        *[P()] * 11,
    )
    out_specs = (P(None, both), P("aa", None))
    return jax.shard_map(
        on_device, mesh=mesh, in_specs=in_specs, out_specs=out_specs, check_vma=False
    )
```

```python
import functools

import jax
import jax.numpy as jnp
from jax import lax
from jax.experimental import pallas as pl
from jax.experimental.pallas import tpu as pltpu
from jax.sharding import PartitionSpec as P

D = 768
HEADS = 16
HEAD_DIM = D // HEADS
BF = jnp.bfloat16
F32 = jnp.float32
MIB = 1 << 20


def dot(a, b, dims=((1,), (0,)), **kw):
    return lax.dot_general(a, b, (dims, ((), ())), preferred_element_type=F32, **kw)


def norm_rows(values, gain_row):
    mean_value = jnp.mean(values, axis=-1, keepdims=True)
    centered = values - mean_value
    variance = jnp.mean(centered * centered, axis=-1, keepdims=True)
    return centered * lax.rsqrt(variance + 1e-05) * gain_row


def whole(n):
    return [pl.BlockSpec(memory_space=pltpu.VMEM)] * n


def state_kernel(tok_rows, cond_ref, pos_ref, noise_ref, ids_ref, w_pos_ref, state_ref, packed_ref):
    atoms = cond_ref.shape[0]
    sigma = noise_ref[0]
    sigma = jnp.full((1, 128), sigma, F32)
    inv = 1.0 / jnp.sqrt(sigma * sigma + 1.0)
    pos = jnp.transpose(
        jnp.concatenate([pos_ref[...] * inv[:, :1], jnp.zeros((5, atoms), F32)], axis=0)
    )
    state = cond_ref[...] + pos[:, 0:1] * w_pos_ref[0:1, :]
    state = state + pos[:, 1:2] * w_pos_ref[1:2, :]
    state = state + pos[:, 2:3] * w_pos_ref[2:3, :]
    state_ref[...] = state
    ids = (ids_ref[...] - lax.axis_index("aa") * tok_rows).astype(F32)
    first = ids[:, :128]
    second = jnp.concatenate([ids[:, 128:], jnp.zeros((1, 256 - atoms), F32)], axis=1)
    tail = jnp.concatenate([first, second, jnp.zeros((14, 128), F32)], axis=0).astype(BF)
    rounded = state.astype(BF)
    for piece in range(packed_ref.shape[0]):
        packed_ref[piece, :atoms, :] = rounded
        packed_ref[piece, atoms:, :] = tail


def bias_kernel(pair_ref, w_ref, out_ref, pair_vmem, held, tops, sems):
    tok_rows, cols, chans = pair_ref.shape
    rows = pair_vmem.shape[1]
    half = rows // 2
    parts = tok_rows // rows

    def arrival(part):
        return pltpu.make_async_copy(
            pair_ref.at[pl.ds(part * rows, rows)], pair_vmem.at[part], sems.at[part]
        )

    for part in range(parts):
        arrival(part).start()
    zeros = jnp.zeros((HEADS, chans), BF)
    weight = w_ref[...]
    weight = jnp.concatenate(
        [
            jnp.concatenate([weight, zeros], axis=1),
            jnp.concatenate([zeros, weight], axis=1),
        ],
        axis=0,
    )
    lanes = lax.broadcasted_iota(jnp.int32, (rows, 128), 1)
    for part in range(parts):
        arrival(part).wait()
        both = jnp.concatenate(
            [
                pair_vmem[part, :half].reshape(half * cols, chans),
                pair_vmem[part, half:].reshape(half * cols, chans),
            ],
            axis=1,
        )
        bias = dot(weight, both, ((1,), (1,)))
        at = (part % 2) * HEADS * rows
        for i in range(half):
            here = slice(i * cols, (i + 1) * cols)
            held[pl.ds(at + i, HEADS, stride=rows), :] = bias[:HEADS, here]
            held[pl.ds(at + half + i, HEADS, stride=rows), :] = bias[HEADS:, here]
        top_of = jnp.zeros((rows, 128), F32)
        for h in range(HEADS):
            lines = held[at + h * rows : at + (h + 1) * rows, :]
            top = jnp.max(lines, axis=1, keepdims=True)
            out_ref[h, part * rows : (part + 1) * rows, :] = (lines - top).astype(BF)
            top_of = jnp.where(lanes == h, top, top_of)
        tops[part * rows : (part + 1) * rows, :] = top_of
    top = jnp.transpose(tops[...])[:HEADS]
    high = top.astype(BF).astype(F32)
    rest = top - high
    middle = rest.astype(BF).astype(F32)
    low = rest - middle
    pad = jnp.zeros((16 - 3 * tok_rows // 128, 128), F32)
    for h in range(HEADS):
        lines = [
            term[h : h + 1, r : r + 128]
            for term in (high, middle, low)
            for r in range(0, tok_rows, 128)
        ]
        out_ref[h, tok_rows:, :] = jnp.concatenate([*lines, pad], axis=0).astype(BF)


def token_kernel(
    mine_ref, other_ref, w_atom_ref, cond_ref, gains_ref, w_head_ref,
    start_ref, query_ref, gate_ref, kv_ref, hidden_ref,
):
    tok_rows = cond_ref.shape[0]
    atoms = mine_ref.shape[1] - 16
    ids = []
    for at, ref in enumerate((mine_ref, other_ref)):
        for piece in range(ref.shape[0]):
            hidden = jax.nn.relu(dot(ref[piece, :atoms, :], w_atom_ref[...]))
            row = (at * ref.shape[0] + piece) * atoms
            hidden_ref[row : row + atoms, :] = hidden.astype(BF)
            tail = ref[piece, atoms:, :].astype(F32)
            ids += [tail[0:1, :], tail[1:2, : atoms - 128]]
    ids = jnp.concatenate(ids, axis=1)
    tokens = lax.broadcasted_iota(jnp.int32, (tok_rows, ids.shape[1]), 0).astype(F32)
    chosen = jnp.where(ids == tokens, 1.0, 0.0)
    counts = jnp.sum(chosen, axis=1, keepdims=True)
    start = cond_ref[...] + dot(chosen.astype(BF), hidden_ref[...]) / counts
    start_ref[...] = start
    normed = norm_rows(start, gains_ref[0:1, :]).astype(BF)
    projected = dot(normed, w_head_ref[...])
    query_ref[...] = projected[:, :HEAD_DIM].astype(BF)
    gate_ref[...] = jax.nn.sigmoid(projected[:, 128 : 128 + HEAD_DIM]).astype(BF)
    kv = jnp.transpose(projected[:, 256:512])
    kv = jnp.concatenate([kv[:HEAD_DIM], kv[128 : 128 + HEAD_DIM]], axis=0).astype(BF)
    kv_ref[...] = kv


def attend_kernel(query_ref, gate_ref, bias_ref, *refs):
    kv_refs, mixed_ref = refs[:-1], refs[-1]
    groups = len(kv_refs)
    keys = kv_refs[0].shape[1]
    tok_rows = query_ref.shape[0]
    me = lax.axis_index("aa")
    per = keys // bias_ref.shape[2]
    order = [
        lax.bitwise_xor(me, g) * per + b for g in range(groups) for b in range(per)
    ]
    tops = []
    for at in order:
        tail = bias_ref[at, tok_rows:, :].astype(F32)
        n = tok_rows // 128
        lines = tail[:n] + tail[n : 2 * n] + tail[2 * n : 3 * n]
        tops.append(jnp.concatenate([lines[i : i + 1] for i in range(n)], axis=1))
    tops = jnp.transpose(jnp.concatenate(tops, axis=0))
    step = 64
    parts = []
    for r in range(0, tok_rows, step):
        query = query_ref[r : r + step, :]
        scores = jnp.concatenate(
            [dot(query, ref[:HEAD_DIM, :]) for ref in kv_refs], axis=1
        ) * HEAD_DIM ** (-0.5)
        bias = jnp.concatenate(
            [
                bias_ref[at, r : r + step, :].astype(F32) + tops[r : r + step, i : i + 1]
                for i, at in enumerate(order)
            ],
            axis=1,
        )
        scores = scores + bias
        top = jnp.max(scores, axis=1, keepdims=True)
        weights = jnp.exp(scores - top)
        total = jnp.sum(weights, axis=1, keepdims=True)
        rounded = weights.astype(BF)
        out = jnp.zeros((step, HEAD_DIM), F32)
        for g in range(groups):
            out += dot(
                rounded[:, g * keys : (g + 1) * keys], kv_refs[g][HEAD_DIM:, :], ((1,), (1,))
            )
        parts.append(out / total)
    attended = jnp.concatenate(parts, axis=0)
    mixed = attended * gate_ref[...].astype(F32)
    mixed = jnp.concatenate([mixed, jnp.zeros((tok_rows, 128 - HEAD_DIM), F32)], axis=1)
    turned = jnp.transpose(mixed)[:HEAD_DIM].astype(BF)
    for piece in range(mixed_ref.shape[0]):
        mixed_ref[piece] = turned


def close_kernel(
    mine_ref, other_ref, w_out_ref, start_ref, gains_ref, w_up_ref, w_down_ref, w_tok_ref,
    state_ref, ids_ref, w_pos_ref, pos_ref, noise_ref,
    denoised_ref, token_ref,
):
    core = lax.rem(lax.axis_index("ba"), 2)
    tok_rows = start_ref.shape[0]
    pieces = mine_ref.shape[0]
    width = pieces * HEAD_DIM
    mine = mine_ref[...].reshape(width, tok_rows)
    other = other_ref[...].reshape(width, tok_rows)
    added = dot(mine, w_out_ref[:, core].reshape(width, D), ((0,), (0,)))
    added += dot(other, w_out_ref[:, 1 - core].reshape(width, D), ((0,), (0,)))
    mid = start_ref[...] + added
    normed = norm_rows(mid, gains_ref[1:2, :]).astype(BF)
    hidden = w_down_ref.shape[0]
    first = dot(normed, w_up_ref[:, :hidden])
    second = dot(normed, w_up_ref[:, hidden:])
    inner = (jax.nn.silu(first) * second).astype(BF)
    token_out = mid + dot(inner, w_down_ref[...])
    token_ref[...] = token_out
    normed = norm_rows(token_out, gains_ref[2:3, :]).astype(BF)
    token_atom = dot(normed, w_tok_ref[...]).astype(BF)
    atoms = state_ref.shape[0]
    tokens = lax.broadcasted_iota(jnp.int32, (tok_rows, atoms), 0)
    tokens += lax.axis_index("aa") * tok_rows
    chosen = jnp.where(ids_ref[...] == tokens, 1.0, 0.0).astype(BF)
    final = state_ref[...] + dot(chosen, token_atom, ((0,), (0,)))
    normed = norm_rows(final, 1.0).astype(BF)
    update = dot(w_pos_ref[...], normed, ((1,), (1,)))
    sigma = jnp.full((1, 128), noise_ref[0], F32)
    inv = (1.0 / jnp.sqrt(sigma * sigma + 1.0))[:, :1]
    denoised_ref[...] = pos_ref[...] * (inv * inv) + update * (sigma[:, :1] * inv)


def shape(dims, dtype):
    return jax.ShapeDtypeStruct(dims, dtype)


def on_device(
    atom_cond, noisy_pos, noise_level, atom_token, token_cond, pair, pair_bias_weight, gains,
    w_pos, w_atom_token, w_query_gate, w_key_value, w_attn_out, w_up, w_down, w_token_atom,
    w_pos_out,
):
    atoms, chans = atom_cond.shape
    tok_rows = token_cond.shape[0]
    cols = pair.shape[1]
    size = lax.axis_size("ba")
    peers = size // 2
    groups = lax.axis_size("aa")
    head = lax.axis_index("ba")
    same_core = [list(range(core, size, 2)) for core in range(2)]
    siblings = [(i, i ^ 1) for i in range(size)]
    smem = pl.BlockSpec(memory_space=pltpu.SMEM)

    def gathered(copies):
        mine = lax.all_to_all(copies, "ba", 0, 0, tiled=True, axis_index_groups=same_core)
        return mine, lax.ppermute(mine, "ba", siblings)

    ids = atom_token[None, :]
    state, packed = pl.pallas_call(
        functools.partial(state_kernel, tok_rows),
        out_shape=(shape((atoms, chans), F32), shape((peers, atoms + 16, chans), BF)),
        in_specs=[*whole(2), smem, *whole(2)],
        out_specs=tuple(whole(2)),
        name="state",
    )(atom_cond, noisy_pos, noise_level, ids, w_pos)

    block = 32
    bias = pl.pallas_call(
        bias_kernel,
        out_shape=shape((HEADS, tok_rows + 16, cols), BF),
        in_specs=[pl.BlockSpec(memory_space=pl.ANY), *whole(1)],
        out_specs=whole(1)[0],
        scratch_shapes=[
            pltpu.VMEM((tok_rows // block, block, cols, chans), BF),
            pltpu.VMEM((2 * HEADS * block, cols), F32),
            pltpu.VMEM((tok_rows, 128), F32),
            pltpu.SemaphoreType.DMA((tok_rows // block,)),
        ],
        compiler_params=pltpu.CompilerParams(vmem_limit_bytes=57 * MIB),
        cost_estimate=pl.CostEstimate(
            flops=2 * tok_rows * cols * chans * 256, bytes_accessed=pair.size * 2 + 2 * MIB,
            transcendentals=0,
        ),
        name="bias",
    )(pair, pair_bias_weight)
    bias = lax.all_to_all(bias, "ba", 0, 0, tiled=True).astype(F32)

    def column(w, at):
        part = lax.dynamic_slice_in_dim(w, at, HEAD_DIM, 1)
        return jnp.pad(part, ((0, 0), (0, 128 - HEAD_DIM)))

    w_head = jnp.concatenate(
        [
            column(w_query_gate, head * HEAD_DIM),
            column(w_query_gate, D + head * HEAD_DIM),
            column(w_key_value, head * HEAD_DIM),
            column(w_key_value, D + head * HEAD_DIM),
        ],
        axis=1,
    )

    mine, other = gathered(packed)
    start, query, gate, kv = pl.pallas_call(
        token_kernel,
        out_shape=(
            shape((tok_rows, D), F32),
            shape((tok_rows, HEAD_DIM), BF),
            shape((tok_rows, HEAD_DIM), BF),
            shape((2 * HEAD_DIM, tok_rows), BF),
        ),
        in_specs=whole(6),
        out_specs=tuple(whole(4)),
        scratch_shapes=[pltpu.VMEM((size * atoms, D), BF)],
        compiler_params=pltpu.CompilerParams(vmem_limit_bytes=24 * MIB),
        name="token",
    )(mine, other, w_atom_token, token_cond, gains, w_head)
    spread = [kv]
    for far in range(1, groups):
        spread.append(lax.ppermute(kv, "aa", [(i, i ^ far) for i in range(groups)]))

    mixed = pl.pallas_call(
        attend_kernel,
        out_shape=shape((peers, HEAD_DIM, tok_rows), BF),
        in_specs=whole(3 + groups),
        out_specs=whole(1)[0],
        compiler_params=pltpu.CompilerParams(vmem_limit_bytes=16 * MIB),
        cost_estimate=pl.CostEstimate(
            flops=20_000_000_000, bytes_accessed=8 * MIB, transcendentals=0
        ),
        name="attend",
    )(query, gate, bias, *spread)
    mine, other = gathered(mixed)

    return pl.pallas_call(
        close_kernel,
        out_shape=(shape((3, atoms), F32), shape((tok_rows, D), F32)),
        in_specs=[*whole(12), smem],
        out_specs=tuple(whole(2)),
        compiler_params=pltpu.CompilerParams(vmem_limit_bytes=24 * MIB),
        name="close",
    )(
        mine, other, w_attn_out.reshape(peers, 2, HEAD_DIM, D), start, gains, w_up, w_down,
        w_token_atom, state, ids, w_pos_out, noisy_pos, noise_level,
    )


def solution(mesh):
    both = ("aa", "ba")
    in_specs = (
        P(both, None), P(None, both), P(), P(both), P("aa", None), P("aa", "ba", None),
        *[P()] * 11,
    )
    out_specs = (P(None, both), P("aa", None))
    return jax.shard_map(
        on_device, mesh=mesh, in_specs=in_specs, out_specs=out_specs, check_vma=False
    )
```

```python
import functools

import jax
import jax.numpy as jnp
from jax import lax
from jax.experimental import pallas as pl
from jax.experimental.pallas import tpu as pltpu
from jax.sharding import PartitionSpec as P

D = 768
HEADS = 16
HEAD_DIM = D // HEADS
DUO = 2 * HEAD_DIM
BF = jnp.bfloat16
F32 = jnp.float32
MIB = 1 << 20


def dot(a, b, dims=((1,), (0,)), **kw):
    return lax.dot_general(a, b, (dims, ((), ())), preferred_element_type=F32, **kw)


def norm_rows(values, gain_row):
    mean_value = jnp.mean(values, axis=-1, keepdims=True)
    centered = values - mean_value
    variance = jnp.mean(centered * centered, axis=-1, keepdims=True)
    return centered * lax.rsqrt(variance + 1e-05) * gain_row


def three(values):
    high = values.astype(BF).astype(F32)
    rest = values - high
    middle = rest.astype(BF).astype(F32)
    return high, middle, rest - middle


def whole(n):
    return [pl.BlockSpec(memory_space=pltpu.VMEM)] * n


def state_kernel(tok_rows, cond_ref, pos_ref, noise_ref, ids_ref, w_pos_ref, state_ref, packed_ref):
    atoms = cond_ref.shape[0]
    sigma = noise_ref[...]
    inv = 1.0 / jnp.sqrt(sigma * sigma + 1.0)
    pos = jnp.transpose(
        jnp.concatenate([pos_ref[...] * inv, jnp.zeros((5, atoms), F32)], axis=0)
    )
    state = cond_ref[...] + pos[:, 0:1] * w_pos_ref[0:1, :]
    state = state + pos[:, 1:2] * w_pos_ref[1:2, :]
    state = state + pos[:, 2:3] * w_pos_ref[2:3, :]
    state_ref[...] = state
    ids = (ids_ref[...] - lax.axis_index("aa") * tok_rows).astype(F32)
    first = ids[:, :128]
    second = jnp.concatenate([ids[:, 128:], jnp.zeros((1, 256 - atoms), F32)], axis=1)
    tail = jnp.concatenate([first, second, jnp.zeros((14, 128), F32)], axis=0).astype(BF)
    rounded = state.astype(BF)
    for piece in range(packed_ref.shape[0]):
        packed_ref[piece, :atoms, :] = rounded
        packed_ref[piece, atoms:, :] = tail


def bias_kernel(pair_ref, w_ref, out_ref, pair_vmem, held, tops, sems):
    tok_rows, cols, chans = pair_ref.shape
    rows = pair_vmem.shape[1]
    half = rows // 2
    parts = tok_rows // rows
    span = tok_rows + 16

    def arrival(part):
        return pltpu.make_async_copy(
            pair_ref.at[pl.ds(part * rows, rows)], pair_vmem.at[part], sems.at[part]
        )

    for part in range(parts):
        arrival(part).start()
    zeros = jnp.zeros((HEADS, chans), BF)
    weight = w_ref[...]
    weight = jnp.concatenate(
        [
            jnp.concatenate([weight, zeros], axis=1),
            jnp.concatenate([zeros, weight], axis=1),
        ],
        axis=0,
    )
    lanes = lax.broadcasted_iota(jnp.int32, (rows, 128), 1)
    for part in range(parts):
        arrival(part).wait()
        both = jnp.concatenate(
            [
                pair_vmem[part, :half].reshape(half * cols, chans),
                pair_vmem[part, half:].reshape(half * cols, chans),
            ],
            axis=1,
        )
        bias = dot(weight, both, ((1,), (1,)))
        at = (part % 2) * HEADS * rows
        for i in range(half):
            here = slice(i * cols, (i + 1) * cols)
            held[pl.ds(at + i, HEADS, stride=rows), :] = bias[:HEADS, here]
            held[pl.ds(at + half + i, HEADS, stride=rows), :] = bias[HEADS:, here]
        top_of = jnp.zeros((rows, 128), F32)
        for h in range(HEADS):
            lines = held[at + h * rows : at + (h + 1) * rows, :]
            top = jnp.max(lines, axis=1, keepdims=True)
            first = h % 2 * span + part * rows
            out_ref[h // 2, first : first + rows, :] = (lines - top).astype(BF)
            top_of = jnp.where(lanes == h, top, top_of)
        tops[part * rows : (part + 1) * rows, :] = top_of
    top = jnp.transpose(tops[...])[:HEADS]
    high, middle, low = three(top)
    pad = jnp.zeros((16 - 3 * tok_rows // 128, 128), F32)
    for h in range(HEADS):
        lines = [
            term[h : h + 1, r : r + 128]
            for term in (high, middle, low)
            for r in range(0, tok_rows, 128)
        ]
        first = h % 2 * span + tok_rows
        out_ref[h // 2, first : first + 16, :] = jnp.concatenate([*lines, pad], axis=0).astype(BF)


def token_kernel(
    mine_ref, other_ref, w_atom_ref, cond_ref, gains_ref, w_head_ref,
    start_ref, query_ref, gate_ref, kv_ref, hidden_ref,
):
    tok_rows = cond_ref.shape[0]
    atoms = mine_ref.shape[1] - 16
    ids = []
    for at, ref in enumerate((mine_ref, other_ref)):
        for piece in range(ref.shape[0]):
            hidden = jax.nn.relu(dot(ref[piece, :atoms, :], w_atom_ref[...]))
            row = (at * ref.shape[0] + piece) * atoms
            hidden_ref[row : row + atoms, :] = hidden.astype(BF)
            tail = ref[piece, atoms:, :].astype(F32)
            ids += [tail[0:1, :], tail[1:2, : atoms - 128]]
    ids = jnp.concatenate(ids, axis=1)
    tokens = lax.broadcasted_iota(jnp.int32, (tok_rows, ids.shape[1]), 0).astype(F32)
    chosen = jnp.where(ids == tokens, 1.0, 0.0)
    counts = jnp.sum(chosen, axis=1, keepdims=True)
    start = cond_ref[...] + dot(chosen.astype(BF), hidden_ref[...]) / counts
    start_ref[...] = start
    normed = norm_rows(start, gains_ref[0:1, :]).astype(BF)
    projected = dot(normed, w_head_ref[...])
    query_ref[...] = projected[:, :DUO].astype(BF)
    gate_ref[...] = jax.nn.sigmoid(projected[:, 128 : 128 + DUO]).astype(BF)
    kv = jnp.transpose(projected[:, 256:512])
    kv = jnp.concatenate([kv[:DUO], kv[128 : 128 + DUO]], axis=0).astype(BF)
    kv_ref[...] = kv


def attend_kernel(query_ref, gate_ref, bias_ref, *refs):
    kv_refs, mixed_ref = refs[:-1], refs[-1]
    ring = len(kv_refs)
    keys = kv_refs[0].shape[1]
    tok_rows = query_ref.shape[0]
    span = tok_rows + 16
    place = lax.rem(lax.axis_index("aa"), ring)
    per = keys // bias_ref.shape[2]
    order = [
        lax.rem(place - by + ring, ring) * per + b for by in range(ring) for b in range(per)
    ]
    n = tok_rows // 128
    step = 128
    outs, stats = [], []
    for j in range(2):
        mine = slice(j * HEAD_DIM, (j + 1) * HEAD_DIM)
        tops = []
        for at in order:
            tail = bias_ref[at, j * span + tok_rows : (j + 1) * span, :]
            lines = tail[:n] + tail[n : 2 * n] + tail[2 * n : 3 * n]
            tops.append(jnp.concatenate([lines[i : i + 1] for i in range(n)], axis=1))
        tops = jnp.transpose(jnp.concatenate(tops, axis=0))
        parts, largest, totals = [], [], []
        for r in range(0, tok_rows, step):
            query = query_ref[r : r + step, mine]
            scores = jnp.concatenate(
                [dot(query, ref[mine, :]) for ref in kv_refs], axis=1
            ) * HEAD_DIM ** (-0.5)
            first = j * span + r
            bias = jnp.concatenate(
                [
                    bias_ref[at, first : first + step, :] + tops[r : r + step, i : i + 1]
                    for i, at in enumerate(order)
                ],
                axis=1,
            )
            scores = scores + bias
            top = jnp.max(scores, axis=1, keepdims=True)
            weights = jnp.exp(scores - top)
            totals.append(jnp.sum(weights, axis=1, keepdims=True))
            largest.append(top)
            rounded = weights.astype(BF)
            out = jnp.zeros((step, HEAD_DIM), F32)
            for g, ref in enumerate(kv_refs):
                values = ref[DUO + j * HEAD_DIM : DUO + (j + 1) * HEAD_DIM, :]
                out += dot(rounded[:, g * keys : (g + 1) * keys], values, ((1,), (1,)))
            parts.append(out)
        outs.append(jnp.concatenate(parts, axis=0))
        stats += [jnp.concatenate(largest, axis=0), jnp.concatenate(totals, axis=0)]
    gated = jnp.concatenate(outs, axis=1) * gate_ref[...].astype(F32)
    spare = jnp.zeros((tok_rows, 128 - DUO - len(stats)), F32)
    turned = jnp.transpose(jnp.concatenate([gated, *stats, spare], axis=1))
    terms = three(turned[DUO : DUO + 4])
    sent = jnp.concatenate([turned[:DUO], *terms, jnp.zeros((4, tok_rows), F32)], axis=0)
    sent = sent.astype(BF)
    for piece in range(mixed_ref.shape[0]):
        mixed_ref[piece] = sent


def joined(ref):
    half = ref.shape[0] // 2
    mixed = []
    for x in range(half):
        pair = (ref[x], ref[half + x])
        stats = []
        for part in pair:
            tail = part[DUO:].astype(F32)
            stats.append(tail[0:4] + tail[4:8] + tail[8:12])
        for j in range(2):
            tops = [st[2 * j : 2 * j + 1] for st in stats]
            overall = jnp.maximum(*tops)
            factors = [jnp.exp(top - overall) for top in tops]
            total = sum(f * st[2 * j + 1 : 2 * j + 2] for f, st in zip(factors, stats))
            mixed.append(
                sum(
                    part[j * HEAD_DIM : (j + 1) * HEAD_DIM].astype(F32) * (f / total)
                    for part, f in zip(pair, factors)
                ).astype(BF)
            )
    return jnp.concatenate(mixed, axis=0)


def close_kernel(
    mine_ref, other_ref, w_out_ref, start_ref, gains_ref, w_up_ref, w_down_ref, w_tok_ref,
    state_ref, ids_ref, w_pos_ref, pos_ref, noise_ref,
    denoised_ref, token_ref,
):
    core = lax.rem(lax.axis_index("ba"), 2)
    tok_rows = start_ref.shape[0]
    pieces = mine_ref.shape[0]
    depth = pieces * HEAD_DIM
    added = dot(joined(mine_ref), w_out_ref[:, core].reshape(depth, D), ((0,), (0,)))
    added += dot(joined(other_ref), w_out_ref[:, 1 - core].reshape(depth, D), ((0,), (0,)))
    mid = start_ref[...] + added
    normed = norm_rows(mid, gains_ref[1:2, :]).astype(BF)
    hidden = w_down_ref.shape[0]
    first = dot(normed, w_up_ref[:, :hidden])
    second = dot(normed, w_up_ref[:, hidden:])
    inner = (jax.nn.silu(first) * second).astype(BF)
    token_out = mid + dot(inner, w_down_ref[...])
    token_ref[...] = token_out
    normed = norm_rows(token_out, gains_ref[2:3, :]).astype(BF)
    token_atom = dot(normed, w_tok_ref[...]).astype(BF)
    atoms = state_ref.shape[0]
    tokens = lax.broadcasted_iota(jnp.int32, (tok_rows, atoms), 0)
    tokens += lax.axis_index("aa") * tok_rows
    chosen = jnp.where(ids_ref[...] == tokens, 1.0, 0.0).astype(BF)
    final = state_ref[...] + dot(chosen, token_atom, ((0,), (0,)))
    normed = norm_rows(final, 1.0).astype(BF)
    update = dot(w_pos_ref[...], normed, ((1,), (1,)))
    sigma = noise_ref[...]
    inv = 1.0 / jnp.sqrt(sigma * sigma + 1.0)
    denoised_ref[...] = pos_ref[...] * (inv * inv) + update * (sigma * inv)


def shape(dims, dtype):
    return jax.ShapeDtypeStruct(dims, dtype)


def on_device(
    atom_cond, noisy_pos, noise_level, atom_token, token_cond, pair, pair_bias_weight, gains,
    w_pos, w_atom_token, w_query_gate, w_key_value, w_attn_out, w_up, w_down, w_token_atom,
    w_pos_out,
):
    atoms, chans = atom_cond.shape
    tok_rows = token_cond.shape[0]
    cols = pair.shape[1]
    size = lax.axis_size("ba")
    peers = size // 2
    groups = lax.axis_size("aa")
    duo = lax.rem(lax.axis_index("ba"), peers)
    same_core = [list(range(core, size, 2)) for core in range(2)]
    halves = [list(range(peers)), list(range(peers, size))]
    siblings = [(i, i ^ 1) for i in range(size)]

    def gathered(copies):
        mine = lax.all_to_all(copies, "ba", 0, 0, tiled=True, axis_index_groups=same_core)
        return mine, lax.ppermute(mine, "ba", siblings)

    ids = atom_token[None, :]
    noise = noise_level[:, None]
    state, packed = pl.pallas_call(
        functools.partial(state_kernel, tok_rows),
        out_shape=(shape((atoms, chans), F32), shape((peers, atoms + 16, chans), BF)),
        in_specs=whole(5),
        out_specs=tuple(whole(2)),
        name="state",
    )(atom_cond, noisy_pos, noise, ids, w_pos)

    block = 32
    bias = pl.pallas_call(
        bias_kernel,
        out_shape=shape((peers, 2 * (tok_rows + 16), cols), BF),
        in_specs=[pl.BlockSpec(memory_space=pl.ANY), *whole(1)],
        out_specs=whole(1)[0],
        scratch_shapes=[
            pltpu.VMEM((tok_rows // block, block, cols, chans), BF),
            pltpu.VMEM((2 * HEADS * block, cols), F32),
            pltpu.VMEM((tok_rows, 128), F32),
            pltpu.SemaphoreType.DMA((tok_rows // block,)),
        ],
        compiler_params=pltpu.CompilerParams(vmem_limit_bytes=57 * MIB),
        cost_estimate=pl.CostEstimate(
            flops=2 * tok_rows * cols * chans * 256, bytes_accessed=pair.size * 2 + 2 * MIB,
            transcendentals=0,
        ),
        name="bias",
    )(pair, pair_bias_weight)
    bias = lax.all_to_all(
        bias, "ba", 0, 0, tiled=True, axis_index_groups=halves
    ).astype(F32)

    def column(w, at):
        part = lax.dynamic_slice_in_dim(w, at, DUO, 1)
        return jnp.pad(part, ((0, 0), (0, 128 - DUO)))

    w_head = jnp.concatenate(
        [
            column(w_query_gate, duo * DUO),
            column(w_query_gate, D + duo * DUO),
            column(w_key_value, duo * DUO),
            column(w_key_value, D + duo * DUO),
        ],
        axis=1,
    )

    mine, other = gathered(packed)
    start, query, gate, kv = pl.pallas_call(
        token_kernel,
        out_shape=(
            shape((tok_rows, D), F32),
            shape((tok_rows, DUO), BF),
            shape((tok_rows, DUO), BF),
            shape((2 * DUO, tok_rows), BF),
        ),
        in_specs=whole(6),
        out_specs=tuple(whole(4)),
        scratch_shapes=[pltpu.VMEM((size * atoms, D), BF)],
        compiler_params=pltpu.CompilerParams(vmem_limit_bytes=24 * MIB),
        name="token",
    )(mine, other, w_atom_token, token_cond, gains, w_head)
    ring = groups // 2
    spread = []
    for by in range(ring):
        moves = []
        for low in range(2):
            for high in range(2):
                for z in range(ring):
                    for w in range(peers):
                        source = (high * ring + z) * size + low * peers + w
                        target = (low * ring + (z + by) % ring) * size + high * peers + w
                        moves.append((source, target))
        spread.append(lax.ppermute(kv, ("aa", "ba"), moves))

    mixed = pl.pallas_call(
        attend_kernel,
        out_shape=shape((peers, DUO + 16, tok_rows), BF),
        in_specs=whole(3 + ring),
        out_specs=whole(1)[0],
        compiler_params=pltpu.CompilerParams(vmem_limit_bytes=16 * MIB),
        cost_estimate=pl.CostEstimate(
            flops=20_000_000_000, bytes_accessed=8 * MIB, transcendentals=0
        ),
        name="attend",
    )(query, gate, bias, *spread)
    mine, other = gathered(mixed)

    return pl.pallas_call(
        close_kernel,
        out_shape=(shape((3, atoms), F32), shape((tok_rows, D), F32)),
        in_specs=whole(13),
        out_specs=tuple(whole(2)),
        compiler_params=pltpu.CompilerParams(vmem_limit_bytes=24 * MIB),
        name="close",
    )(
        mine, other, w_attn_out.reshape(peers // 2, 2, DUO, D), start, gains, w_up, w_down,
        w_token_atom, state, ids, w_pos_out, noisy_pos, noise,
    )


def solution(mesh):
    both = ("aa", "ba")
    in_specs = (
        P(both, None), P(None, both), P(), P(both), P("aa", None), P("aa", "ba", None),
        *[P()] * 11,
    )
    out_specs = (P(None, both), P("aa", None))
    return jax.shard_map(
        on_device, mesh=mesh, in_specs=in_specs, out_specs=out_specs, check_vma=False
    )
```

```python
import functools

import jax
import jax.numpy as jnp
from jax import lax
from jax.experimental import pallas as pl
from jax.experimental.pallas import tpu as pltpu
from jax.sharding import PartitionSpec as P

D = 768
HEADS = 16
HEAD_DIM = D // HEADS
DUO = 2 * HEAD_DIM
STEPS = (2, 1, 3, 0)
BF = jnp.bfloat16
F32 = jnp.float32
MIB = 1 << 20


def dot(a, b, dims=((1,), (0,)), **kw):
    return lax.dot_general(a, b, (dims, ((), ())), preferred_element_type=F32, **kw)


def norm_rows(values, gain_row):
    mean_value = jnp.mean(values, axis=-1, keepdims=True)
    centered = values - mean_value
    variance = jnp.mean(centered * centered, axis=-1, keepdims=True)
    return centered * lax.rsqrt(variance + 1e-05) * gain_row


def three(values):
    high = values.astype(BF).astype(F32)
    rest = values - high
    middle = rest.astype(BF).astype(F32)
    return high, middle, rest - middle


def whole(n):
    return [pl.BlockSpec(memory_space=pltpu.VMEM)] * n


def state_kernel(tok_rows, cond_ref, pos_ref, noise_ref, ids_ref, w_pos_ref, state_ref, packed_ref):
    atoms = cond_ref.shape[0]
    sigma = noise_ref[...]
    inv = 1.0 / jnp.sqrt(sigma * sigma + 1.0)
    pos = jnp.transpose(
        jnp.concatenate([pos_ref[...] * inv, jnp.zeros((5, atoms), F32)], axis=0)
    )
    state = cond_ref[...] + pos[:, 0:1] * w_pos_ref[0:1, :]
    state = state + pos[:, 1:2] * w_pos_ref[1:2, :]
    state = state + pos[:, 2:3] * w_pos_ref[2:3, :]
    state_ref[...] = state
    ids = (ids_ref[...] - lax.axis_index("aa") * tok_rows).astype(F32)
    first = ids[:, :128]
    second = jnp.concatenate([ids[:, 128:], jnp.zeros((1, 256 - atoms), F32)], axis=1)
    tail = jnp.concatenate([first, second, jnp.zeros((14, 128), F32)], axis=0).astype(BF)
    rounded = state.astype(BF)
    for piece in range(packed_ref.shape[0]):
        packed_ref[piece, :atoms, :] = rounded
        packed_ref[piece, atoms:, :] = tail


def bias_kernel(pair_ref, w_ref, out_ref, pair_vmem, held, tops, sems):
    tok_rows, cols, chans = pair_ref.shape
    rows = pair_vmem.shape[1]
    half = rows // 2
    parts = tok_rows // rows
    span = tok_rows + 16

    def arrival(part):
        return pltpu.make_async_copy(
            pair_ref.at[pl.ds(part * rows, rows)], pair_vmem.at[part], sems.at[part]
        )

    for part in range(parts):
        arrival(part).start()
    zeros = jnp.zeros((HEADS, chans), BF)
    weight = w_ref[...]
    weight = jnp.concatenate(
        [
            jnp.concatenate([weight, zeros], axis=1),
            jnp.concatenate([zeros, weight], axis=1),
        ],
        axis=0,
    )
    lanes = lax.broadcasted_iota(jnp.int32, (rows, 128), 1)
    for part in range(parts):
        arrival(part).wait()
        both = jnp.concatenate(
            [
                pair_vmem[part, :half].reshape(half * cols, chans),
                pair_vmem[part, half:].reshape(half * cols, chans),
            ],
            axis=1,
        )
        bias = dot(weight, both, ((1,), (1,)))
        step = rows + 8
        at = (part % 2) * HEADS * step
        for i in range(half):
            here = slice(i * cols, (i + 1) * cols)
            held[pl.ds(at + i, HEADS, stride=step), :] = bias[:HEADS, here]
            held[pl.ds(at + half + i, HEADS, stride=step), :] = bias[HEADS:, here]
        top_of = jnp.zeros((rows, 128), F32)
        for h in range(HEADS):
            lines = held[at + h * step : at + h * step + rows, :]
            top = jnp.max(lines, axis=1, keepdims=True)
            first = h % 2 * span + part * rows
            out_ref[h // 2, first : first + rows, :] = (lines - top).astype(BF)
            top_of = jnp.where(lanes == h, top, top_of)
        tops[part * rows : (part + 1) * rows, :] = top_of
    top = jnp.transpose(tops[...])[:HEADS]
    high, middle, low = three(top)
    pad = jnp.zeros((16 - 3 * tok_rows // 128, 128), F32)
    for h in range(HEADS):
        lines = [
            term[h : h + 1, r : r + 128]
            for term in (high, middle, low)
            for r in range(0, tok_rows, 128)
        ]
        first = h % 2 * span + tok_rows
        out_ref[h // 2, first : first + 16, :] = jnp.concatenate([*lines, pad], axis=0).astype(BF)


def token_kernel(
    mine_ref, other_ref, w_atom_ref, cond_ref, gains_ref, w_head_ref,
    start_ref, query_ref, gate_ref, kv_ref, hidden_ref,
):
    tok_rows = cond_ref.shape[0]
    atoms = mine_ref.shape[1] - 16
    ids = []
    for at, ref in enumerate((mine_ref, other_ref)):
        for piece in range(ref.shape[0]):
            hidden = jax.nn.relu(dot(ref[piece, :atoms, :], w_atom_ref[...]))
            row = (at * ref.shape[0] + piece) * atoms
            hidden_ref[row : row + atoms, :] = hidden.astype(BF)
            tail = ref[piece, atoms:, :].astype(F32)
            ids += [tail[0:1, :], tail[1:2, : atoms - 128]]
    ids = jnp.concatenate(ids, axis=1)
    tokens = lax.broadcasted_iota(jnp.int32, (tok_rows, ids.shape[1]), 0).astype(F32)
    chosen = jnp.where(ids == tokens, 1.0, 0.0)
    counts = jnp.sum(chosen, axis=1, keepdims=True)
    start = cond_ref[...] + dot(chosen.astype(BF), hidden_ref[...]) / counts
    start_ref[...] = start
    normed = norm_rows(start, gains_ref[0:1, :]).astype(BF)
    projected = dot(normed, w_head_ref[...])
    query_ref[...] = projected[:, :DUO].astype(BF)
    gate_ref[...] = jax.nn.sigmoid(projected[:, 128 : 128 + DUO]).astype(BF)
    kv = jnp.transpose(projected[:, 256:512])
    kv = jnp.concatenate([kv[:DUO], kv[128 : 128 + DUO]], axis=0).astype(BF)
    kv_ref[...] = kv


def attend_kernel(query_ref, gate_ref, bias_ref, *refs):
    kv_refs, mixed_ref = refs[:-1], refs[-1]
    ring = len(kv_refs)
    keys = kv_refs[0].shape[1]
    tok_rows = query_ref.shape[0]
    span = tok_rows + 16
    place = lax.rem(lax.axis_index("aa"), ring)
    per = keys // bias_ref.shape[2]
    order = [lax.rem(place - by + ring, ring) * per + b for by in STEPS for b in range(per)]
    n = tok_rows // 128
    step = 128
    outs, stats = [], []
    for j in range(2):
        mine = slice(j * HEAD_DIM, (j + 1) * HEAD_DIM)
        tops = []
        for at in order:
            tail = bias_ref[at, j * span + tok_rows : (j + 1) * span, :]
            lines = tail[:n] + tail[n : 2 * n] + tail[2 * n : 3 * n]
            tops.append(jnp.concatenate([lines[i : i + 1] for i in range(n)], axis=1))
        tops = jnp.transpose(jnp.concatenate(tops, axis=0))
        parts, largest, totals = [], [], []
        for r in range(0, tok_rows, step):
            query = query_ref[r : r + step, mine]
            scores = jnp.concatenate(
                [dot(query, ref[mine, :]) for ref in kv_refs], axis=1
            ) * HEAD_DIM ** (-0.5)
            first = j * span + r
            bias = jnp.concatenate(
                [
                    bias_ref[at, first : first + step, :] + tops[r : r + step, i : i + 1]
                    for i, at in enumerate(order)
                ],
                axis=1,
            )
            scores = scores + bias
            top = jnp.max(scores, axis=1, keepdims=True)
            weights = jnp.exp(scores - top)
            totals.append(jnp.sum(weights, axis=1, keepdims=True))
            largest.append(top)
            rounded = weights.astype(BF)
            out = jnp.zeros((step, HEAD_DIM), F32)
            for g, ref in enumerate(kv_refs):
                values = ref[DUO + j * HEAD_DIM : DUO + (j + 1) * HEAD_DIM, :]
                out += dot(rounded[:, g * keys : (g + 1) * keys], values, ((1,), (1,)))
            parts.append(out)
        outs.append(jnp.concatenate(parts, axis=0))
        stats += [jnp.concatenate(largest, axis=0), jnp.concatenate(totals, axis=0)]
    gated = jnp.concatenate(outs, axis=1) * gate_ref[...].astype(F32)
    spare = jnp.zeros((tok_rows, 128 - DUO - len(stats)), F32)
    turned = jnp.transpose(jnp.concatenate([gated, *stats, spare], axis=1))
    terms = three(turned[DUO : DUO + 4])
    sent = jnp.concatenate([turned[:DUO], *terms, jnp.zeros((4, tok_rows), F32)], axis=0)
    sent = sent.astype(BF)
    for piece in range(mixed_ref.shape[0]):
        mixed_ref[piece] = sent


def joined(ref):
    half = ref.shape[0] // 2
    mixed = []
    for x in range(half):
        pair = (ref[2 * x], ref[2 * x + 1])
        stats = []
        for part in pair:
            tail = part[DUO:].astype(F32)
            stats.append(tail[0:4] + tail[4:8] + tail[8:12])
        for j in range(2):
            tops = [st[2 * j : 2 * j + 1] for st in stats]
            overall = jnp.maximum(*tops)
            factors = [jnp.exp(top - overall) for top in tops]
            total = sum(f * st[2 * j + 1 : 2 * j + 2] for f, st in zip(factors, stats))
            mixed.append(
                sum(
                    part[j * HEAD_DIM : (j + 1) * HEAD_DIM].astype(F32) * (f / total)
                    for part, f in zip(pair, factors)
                ).astype(BF)
            )
    return jnp.concatenate(mixed, axis=0)


def close_kernel(
    mine_ref, other_ref, w_out_ref, start_ref, gains_ref, w_up_ref, w_down_ref, w_tok_ref,
    state_ref, ids_ref, w_pos_ref, pos_ref, noise_ref,
    denoised_ref, token_ref,
):
    core = lax.rem(lax.axis_index("ba"), 2)
    tok_rows = start_ref.shape[0]
    pieces = mine_ref.shape[0]
    depth = pieces * HEAD_DIM
    added = dot(joined(mine_ref), w_out_ref[:, core].reshape(depth, D), ((0,), (0,)))
    added += dot(joined(other_ref), w_out_ref[:, 1 - core].reshape(depth, D), ((0,), (0,)))
    mid = start_ref[...] + added
    normed = norm_rows(mid, gains_ref[1:2, :]).astype(BF)
    hidden = w_down_ref.shape[0]
    first = dot(normed, w_up_ref[:, :hidden])
    second = dot(normed, w_up_ref[:, hidden:])
    inner = (jax.nn.silu(first) * second).astype(BF)
    token_out = mid + dot(inner, w_down_ref[...])
    token_ref[...] = token_out
    normed = norm_rows(token_out, gains_ref[2:3, :]).astype(BF)
    token_atom = dot(normed, w_tok_ref[...]).astype(BF)
    atoms = state_ref.shape[0]
    tokens = lax.broadcasted_iota(jnp.int32, (tok_rows, atoms), 0)
    tokens += lax.axis_index("aa") * tok_rows
    chosen = jnp.where(ids_ref[...] == tokens, 1.0, 0.0).astype(BF)
    final = state_ref[...] + dot(chosen, token_atom, ((0,), (0,)))
    normed = norm_rows(final, 1.0).astype(BF)
    update = dot(w_pos_ref[...], normed, ((1,), (1,)))
    sigma = noise_ref[...]
    inv = 1.0 / jnp.sqrt(sigma * sigma + 1.0)
    denoised_ref[...] = pos_ref[...] * (inv * inv) + update * (sigma * inv)


def shape(dims, dtype):
    return jax.ShapeDtypeStruct(dims, dtype)


def on_device(
    atom_cond, noisy_pos, noise_level, atom_token, token_cond, pair, pair_bias_weight, gains,
    w_pos, w_atom_token, w_query_gate, w_key_value, w_attn_out, w_up, w_down, w_token_atom,
    w_pos_out,
):
    atoms, chans = atom_cond.shape
    tok_rows = token_cond.shape[0]
    cols = pair.shape[1]
    size = lax.axis_size("ba")
    peers = size // 2
    groups = lax.axis_size("aa")
    duo = lax.rem(lax.axis_index("ba"), peers)
    woven = [i + j for i in range(0, peers, 2) for j in (0, peers)]
    same_core = [woven, [(i + peers + 1) % size for i in woven]]
    turned_core = [woven, [(i + 5) % size for i in woven]]
    halves = [list(range(peers)), list(range(peers, size))]
    siblings = [(i, i ^ 1) for i in range(size)]

    def gathered(copies, sets):
        mine = lax.all_to_all(copies, "ba", 0, 0, tiled=True, axis_index_groups=sets)
        return mine, lax.ppermute(mine, "ba", siblings)

    ids = atom_token[None, :]
    noise = noise_level[:, None]
    state, packed = pl.pallas_call(
        functools.partial(state_kernel, tok_rows),
        out_shape=(shape((atoms, chans), F32), shape((peers, atoms + 16, chans), BF)),
        in_specs=whole(5),
        out_specs=tuple(whole(2)),
        name="state",
    )(atom_cond, noisy_pos, noise, ids, w_pos)

    block = 64
    bias = pl.pallas_call(
        bias_kernel,
        out_shape=shape((peers, 2 * (tok_rows + 16), cols), BF),
        in_specs=[pl.BlockSpec(memory_space=pl.ANY), *whole(1)],
        out_specs=whole(1)[0],
        scratch_shapes=[
            pltpu.VMEM((tok_rows // block, block, cols, chans), BF),
            pltpu.VMEM((2 * HEADS * (block + 8), cols), F32),
            pltpu.VMEM((tok_rows, 128), F32),
            pltpu.SemaphoreType.DMA((tok_rows // block,)),
        ],
        compiler_params=pltpu.CompilerParams(vmem_limit_bytes=57 * MIB),
        cost_estimate=pl.CostEstimate(
            flops=2 * tok_rows * cols * chans * 256, bytes_accessed=pair.size * 2 + 2 * MIB,
            transcendentals=0,
        ),
        name="bias",
    )(pair, pair_bias_weight)
    bias = lax.all_to_all(
        bias, "ba", 0, 0, tiled=True, axis_index_groups=halves
    ).astype(F32)

    def column(w, at):
        part = lax.dynamic_slice_in_dim(w, at, DUO, 1)
        return jnp.pad(part, ((0, 0), (0, 128 - DUO)))

    w_head = jnp.concatenate(
        [
            column(w_query_gate, duo * DUO),
            column(w_query_gate, D + duo * DUO),
            column(w_key_value, duo * DUO),
            column(w_key_value, D + duo * DUO),
        ],
        axis=1,
    )

    mine, other = gathered(packed, turned_core)
    start, query, gate, kv = pl.pallas_call(
        token_kernel,
        out_shape=(
            shape((tok_rows, D), F32),
            shape((tok_rows, DUO), BF),
            shape((tok_rows, DUO), BF),
            shape((2 * DUO, tok_rows), BF),
        ),
        in_specs=whole(6),
        out_specs=tuple(whole(4)),
        scratch_shapes=[pltpu.VMEM((size * atoms, D), BF)],
        compiler_params=pltpu.CompilerParams(vmem_limit_bytes=24 * MIB),
        name="token",
    )(mine, other, w_atom_token, token_cond, gains, w_head)
    ring = groups // 2
    spread = []
    for by in STEPS:
        moves = []
        for low in range(2):
            for high in range(2):
                for z in range(ring):
                    for w in range(peers):
                        source = (high * ring + z) * size + low * peers + w
                        target = (low * ring + (z + by) % ring) * size + high * peers + w
                        moves.append((source, target))
        spread.append(lax.ppermute(kv, ("aa", "ba"), moves))

    mixed = pl.pallas_call(
        attend_kernel,
        out_shape=shape((peers, DUO + 16, tok_rows), BF),
        in_specs=whole(3 + ring),
        out_specs=whole(1)[0],
        compiler_params=pltpu.CompilerParams(vmem_limit_bytes=16 * MIB),
        cost_estimate=pl.CostEstimate(
            flops=20_000_000_000, bytes_accessed=8 * MIB, transcendentals=0
        ),
        name="attend",
    )(query, gate, bias, *spread)
    mine, other = gathered(mixed, same_core)

    return pl.pallas_call(
        close_kernel,
        out_shape=(shape((3, atoms), F32), shape((tok_rows, D), F32)),
        in_specs=whole(13),
        out_specs=tuple(whole(2)),
        compiler_params=pltpu.CompilerParams(vmem_limit_bytes=24 * MIB),
        name="close",
    )(
        mine, other, w_attn_out.reshape(peers // 2, 2, DUO, D), start, gains, w_up, w_down,
        w_token_atom, state, ids, w_pos_out, noisy_pos, noise,
    )


def solution(mesh):
    both = ("aa", "ba")
    in_specs = (
        P(both, None), P(None, both), P(), P(both), P("aa", None), P("aa", "ba", None),
        *[P()] * 11,
    )
    out_specs = (P(None, both), P("aa", None))
    return jax.shard_map(
        on_device, mesh=mesh, in_specs=in_specs, out_specs=out_specs, check_vma=False
    )
```

```python
import functools

import jax
import jax.numpy as jnp
from jax import lax
from jax.experimental import pallas as pl
from jax.experimental.pallas import tpu as pltpu
from jax.sharding import PartitionSpec as P

D = 768
HEADS = 16
HEAD_DIM = D // HEADS
DUO = 2 * HEAD_DIM
STEPS = (2, 3, 1, 0)
BF = jnp.bfloat16
F32 = jnp.float32
MIB = 1 << 20


def dot(a, b, dims=((1,), (0,)), **kw):
    return lax.dot_general(a, b, (dims, ((), ())), preferred_element_type=F32, **kw)


def norm_rows(values, gain_row):
    mean_value = jnp.mean(values, axis=-1, keepdims=True)
    centered = values - mean_value
    variance = jnp.mean(centered * centered, axis=-1, keepdims=True)
    return centered * lax.rsqrt(variance + 1e-05) * gain_row


def three(values):
    high = values.astype(BF).astype(F32)
    rest = values - high
    middle = rest.astype(BF).astype(F32)
    return high, middle, rest - middle


def whole(n):
    return [pl.BlockSpec(memory_space=pltpu.VMEM)] * n


def state_kernel(tok_rows, cond_ref, pos_ref, noise_ref, ids_ref, w_pos_ref, state_ref, packed_ref):
    atoms = cond_ref.shape[0]
    sigma = noise_ref[...]
    inv = 1.0 / jnp.sqrt(sigma * sigma + 1.0)
    pos = jnp.transpose(
        jnp.concatenate([pos_ref[...] * inv, jnp.zeros((5, atoms), F32)], axis=0)
    )
    state = cond_ref[...] + pos[:, 0:1] * w_pos_ref[0:1, :]
    state = state + pos[:, 1:2] * w_pos_ref[1:2, :]
    state = state + pos[:, 2:3] * w_pos_ref[2:3, :]
    state_ref[...] = state
    ids = (ids_ref[...] - lax.axis_index("aa") * tok_rows).astype(F32)
    first = ids[:, :128]
    second = jnp.concatenate([ids[:, 128:], jnp.zeros((1, 256 - atoms), F32)], axis=1)
    tail = jnp.concatenate([first, second, jnp.zeros((14, 128), F32)], axis=0).astype(BF)
    rounded = state.astype(BF)
    for piece in range(packed_ref.shape[0]):
        packed_ref[piece, :atoms, :] = rounded
        packed_ref[piece, atoms:, :] = tail


def bias_kernel(pair_ref, w_ref, out_ref, pair_vmem, held, tops, sems):
    tok_rows, cols, chans = pair_ref.shape
    rows = pair_vmem.shape[1]
    half = rows // 2
    parts = tok_rows // rows
    span = tok_rows + 16

    def arrival(part):
        return pltpu.make_async_copy(
            pair_ref.at[pl.ds(part * rows, rows)], pair_vmem.at[part], sems.at[part]
        )

    for part in range(parts):
        arrival(part).start()
    zeros = jnp.zeros((HEADS, chans), BF)
    weight = w_ref[...]
    weight = jnp.concatenate(
        [
            jnp.concatenate([weight, zeros], axis=1),
            jnp.concatenate([zeros, weight], axis=1),
        ],
        axis=0,
    )
    lanes = lax.broadcasted_iota(jnp.int32, (rows, 128), 1)
    for part in range(parts):
        arrival(part).wait()
        both = jnp.concatenate(
            [
                pair_vmem[part, :half].reshape(half * cols, chans),
                pair_vmem[part, half:].reshape(half * cols, chans),
            ],
            axis=1,
        )
        bias = dot(weight, both, ((1,), (1,)))
        step = rows + 8
        at = (part % 2) * HEADS * step
        for i in range(half):
            here = slice(i * cols, (i + 1) * cols)
            held[pl.ds(at + i, HEADS, stride=step), :] = bias[:HEADS, here]
            held[pl.ds(at + half + i, HEADS, stride=step), :] = bias[HEADS:, here]
        top_of = jnp.zeros((rows, 128), F32)
        for h in range(HEADS):
            lines = held[at + h * step : at + h * step + rows, :]
            top = jnp.max(lines, axis=1, keepdims=True)
            first = h % 2 * span + part * rows
            out_ref[h // 2, first : first + rows, :] = (lines - top).astype(BF)
            top_of = jnp.where(lanes == h, top, top_of)
        tops[part * rows : (part + 1) * rows, :] = top_of
    top = jnp.transpose(tops[...])[:HEADS]
    high, middle, low = three(top)
    pad = jnp.zeros((16 - 3 * tok_rows // 128, 128), F32)
    for h in range(HEADS):
        lines = [
            term[h : h + 1, r : r + 128]
            for term in (high, middle, low)
            for r in range(0, tok_rows, 128)
        ]
        first = h % 2 * span + tok_rows
        out_ref[h // 2, first : first + 16, :] = jnp.concatenate([*lines, pad], axis=0).astype(BF)


def token_kernel(
    mine_ref, other_ref, w_atom_ref, cond_ref, gains_ref, w_head_ref,
    start_ref, query_ref, gate_ref, kv_ref, hidden_ref,
):
    tok_rows = cond_ref.shape[0]
    atoms = mine_ref.shape[1] - 16
    ids = []
    for at, ref in enumerate((mine_ref, other_ref)):
        for piece in range(ref.shape[0]):
            hidden = jax.nn.relu(dot(ref[piece, :atoms, :], w_atom_ref[...]))
            row = (at * ref.shape[0] + piece) * atoms
            hidden_ref[row : row + atoms, :] = hidden.astype(BF)
            tail = ref[piece, atoms:, :].astype(F32)
            ids += [tail[0:1, :], tail[1:2, : atoms - 128]]
    ids = jnp.concatenate(ids, axis=1)
    tokens = lax.broadcasted_iota(jnp.int32, (tok_rows, ids.shape[1]), 0).astype(F32)
    chosen = jnp.where(ids == tokens, 1.0, 0.0)
    counts = jnp.sum(chosen, axis=1, keepdims=True)
    start = cond_ref[...] + dot(chosen.astype(BF), hidden_ref[...]) / counts
    start_ref[...] = start
    normed = norm_rows(start, gains_ref[0:1, :]).astype(BF)
    projected = dot(normed, w_head_ref[...])
    query_ref[...] = projected[:, :DUO].astype(BF)
    gate_ref[...] = jax.nn.sigmoid(projected[:, 128 : 128 + DUO]).astype(BF)
    kv = jnp.transpose(projected[:, 256:512])
    kv = jnp.concatenate([kv[:DUO], kv[128 : 128 + DUO]], axis=0).astype(BF)
    kv_ref[...] = kv


def attend_kernel(query_ref, gate_ref, bias_ref, *refs):
    kv_refs, mixed_ref = refs[:-1], refs[-1]
    ring = len(kv_refs)
    keys = kv_refs[0].shape[1]
    tok_rows = query_ref.shape[0]
    span = tok_rows + 16
    place = lax.rem(lax.axis_index("aa"), ring)
    per = keys // bias_ref.shape[2]
    order = [lax.rem(place - by + ring, ring) * per + b for by in STEPS for b in range(per)]
    n = tok_rows // 128
    step = 128
    outs, stats = [], []
    for j in range(2):
        mine = slice(j * HEAD_DIM, (j + 1) * HEAD_DIM)
        tops = []
        for at in order:
            tail = bias_ref[at, j * span + tok_rows : (j + 1) * span, :]
            lines = tail[:n] + tail[n : 2 * n] + tail[2 * n : 3 * n]
            tops.append(jnp.concatenate([lines[i : i + 1] for i in range(n)], axis=1))
        tops = jnp.transpose(jnp.concatenate(tops, axis=0))
        parts, largest, totals = [], [], []
        for r in range(0, tok_rows, step):
            query = query_ref[r : r + step, mine]
            scores = jnp.concatenate(
                [dot(query, ref[mine, :]) for ref in kv_refs], axis=1
            ) * HEAD_DIM ** (-0.5)
            first = j * span + r
            bias = jnp.concatenate(
                [
                    bias_ref[at, first : first + step, :] + tops[r : r + step, i : i + 1]
                    for i, at in enumerate(order)
                ],
                axis=1,
            )
            scores = scores + bias
            top = jnp.max(scores, axis=1, keepdims=True)
            weights = jnp.exp(scores - top)
            totals.append(jnp.sum(weights, axis=1, keepdims=True))
            largest.append(top)
            rounded = weights.astype(BF)
            out = jnp.zeros((step, HEAD_DIM), F32)
            for g, ref in enumerate(kv_refs):
                values = ref[DUO + j * HEAD_DIM : DUO + (j + 1) * HEAD_DIM, :]
                out += dot(rounded[:, g * keys : (g + 1) * keys], values, ((1,), (1,)))
            parts.append(out)
        outs.append(jnp.concatenate(parts, axis=0))
        stats += [jnp.concatenate(largest, axis=0), jnp.concatenate(totals, axis=0)]
    gated = jnp.concatenate(outs, axis=1) * gate_ref[...].astype(F32)
    spare = jnp.zeros((tok_rows, 128 - DUO - len(stats)), F32)
    turned = jnp.transpose(jnp.concatenate([gated, *stats, spare], axis=1))
    terms = three(turned[DUO : DUO + 4])
    sent = jnp.concatenate([turned[:DUO], *terms, jnp.zeros((4, tok_rows), F32)], axis=0)
    sent = sent.astype(BF)
    for piece in range(mixed_ref.shape[0]):
        mixed_ref[piece] = sent


def joined(ref):
    half = ref.shape[0] // 2
    mixed = []
    for x in range(half):
        pair = (ref[2 * x], ref[2 * x + 1])
        stats = []
        for part in pair:
            tail = part[DUO:].astype(F32)
            stats.append(tail[0:4] + tail[4:8] + tail[8:12])
        for j in range(2):
            tops = [st[2 * j : 2 * j + 1] for st in stats]
            overall = jnp.maximum(*tops)
            factors = [jnp.exp(top - overall) for top in tops]
            total = sum(f * st[2 * j + 1 : 2 * j + 2] for f, st in zip(factors, stats))
            mixed.append(
                sum(
                    part[j * HEAD_DIM : (j + 1) * HEAD_DIM].astype(F32) * (f / total)
                    for part, f in zip(pair, factors)
                ).astype(BF)
            )
    return jnp.concatenate(mixed, axis=0)


def close_kernel(
    mine_ref, other_ref, w_out_ref, start_ref, gains_ref, w_up_ref, w_down_ref, w_tok_ref,
    state_ref, ids_ref, w_pos_ref, pos_ref, noise_ref,
    denoised_ref, token_ref,
):
    core = lax.rem(lax.axis_index("ba"), 2)
    tok_rows = start_ref.shape[0]
    pieces = mine_ref.shape[0]
    depth = pieces * HEAD_DIM
    added = dot(joined(mine_ref), w_out_ref[:, core].reshape(depth, D), ((0,), (0,)))
    added += dot(joined(other_ref), w_out_ref[:, 1 - core].reshape(depth, D), ((0,), (0,)))
    mid = start_ref[...] + added
    normed = norm_rows(mid, gains_ref[1:2, :]).astype(BF)
    hidden = w_down_ref.shape[0]
    first = dot(normed, w_up_ref[:, :hidden])
    second = dot(normed, w_up_ref[:, hidden:])
    inner = (jax.nn.silu(first) * second).astype(BF)
    token_out = mid + dot(inner, w_down_ref[...])
    token_ref[...] = token_out
    normed = norm_rows(token_out, gains_ref[2:3, :]).astype(BF)
    token_atom = dot(normed, w_tok_ref[...]).astype(BF)
    atoms = state_ref.shape[0]
    tokens = lax.broadcasted_iota(jnp.int32, (tok_rows, atoms), 0)
    tokens += lax.axis_index("aa") * tok_rows
    chosen = jnp.where(ids_ref[...] == tokens, 1.0, 0.0).astype(BF)
    final = state_ref[...] + dot(chosen, token_atom, ((0,), (0,)))
    normed = norm_rows(final, 1.0).astype(BF)
    update = dot(w_pos_ref[...], normed, ((1,), (1,)))
    sigma = noise_ref[...]
    inv = 1.0 / jnp.sqrt(sigma * sigma + 1.0)
    denoised_ref[...] = pos_ref[...] * (inv * inv) + update * (sigma * inv)


def shape(dims, dtype):
    return jax.ShapeDtypeStruct(dims, dtype)


def on_device(
    atom_cond, noisy_pos, noise_level, atom_token, token_cond, pair, pair_bias_weight, gains,
    w_pos, w_atom_token, w_query_gate, w_key_value, w_attn_out, w_up, w_down, w_token_atom,
    w_pos_out,
):
    atoms, chans = atom_cond.shape
    tok_rows = token_cond.shape[0]
    cols = pair.shape[1]
    size = lax.axis_size("ba")
    peers = size // 2
    groups = lax.axis_size("aa")
    duo = lax.rem(lax.axis_index("ba"), peers)
    woven = [i + j for i in range(0, peers, 2) for j in (0, peers)]
    same_core = [woven, [(i + peers + 1) % size for i in woven]]
    turned_core = [woven, [(i + 5) % size for i in woven]]
    halves = [list(range(peers)), list(range(peers, size))]
    siblings = [(i, i ^ 1) for i in range(size)]

    def gathered(copies, sets):
        mine = lax.all_to_all(copies, "ba", 0, 0, tiled=True, axis_index_groups=sets)
        return mine, lax.ppermute(mine, "ba", siblings)

    ids = atom_token[None, :]
    noise = noise_level[:, None]
    state, packed = pl.pallas_call(
        functools.partial(state_kernel, tok_rows),
        out_shape=(shape((atoms, chans), F32), shape((peers, atoms + 16, chans), BF)),
        in_specs=whole(5),
        out_specs=tuple(whole(2)),
        name="state",
    )(atom_cond, noisy_pos, noise, ids, w_pos)

    block = 64
    bias = pl.pallas_call(
        bias_kernel,
        out_shape=shape((peers, 2 * (tok_rows + 16), cols), BF),
        in_specs=[pl.BlockSpec(memory_space=pl.ANY), *whole(1)],
        out_specs=whole(1)[0],
        scratch_shapes=[
            pltpu.VMEM((tok_rows // block, block, cols, chans), BF),
            pltpu.VMEM((2 * HEADS * (block + 8), cols), F32),
            pltpu.VMEM((tok_rows, 128), F32),
            pltpu.SemaphoreType.DMA((tok_rows // block,)),
        ],
        compiler_params=pltpu.CompilerParams(vmem_limit_bytes=57 * MIB),
        cost_estimate=pl.CostEstimate(
            flops=2 * tok_rows * cols * chans * 256, bytes_accessed=pair.size * 2 + 2 * MIB,
            transcendentals=0,
        ),
        name="bias",
    )(pair, pair_bias_weight)
    bias = lax.all_to_all(
        bias, "ba", 0, 0, tiled=True, axis_index_groups=halves
    ).astype(F32)

    def column(w, at):
        part = lax.dynamic_slice_in_dim(w, at, DUO, 1)
        return jnp.pad(part, ((0, 0), (0, 128 - DUO)))

    w_head = jnp.concatenate(
        [
            column(w_query_gate, duo * DUO),
            column(w_query_gate, D + duo * DUO),
            column(w_key_value, duo * DUO),
            column(w_key_value, D + duo * DUO),
        ],
        axis=1,
    )

    mine, other = gathered(packed, turned_core)
    start, query, gate, kv = pl.pallas_call(
        token_kernel,
        out_shape=(
            shape((tok_rows, D), F32),
            shape((tok_rows, DUO), BF),
            shape((tok_rows, DUO), BF),
            shape((2 * DUO, tok_rows), BF),
        ),
        in_specs=whole(6),
        out_specs=tuple(whole(4)),
        scratch_shapes=[pltpu.VMEM((size * atoms, D), BF)],
        compiler_params=pltpu.CompilerParams(vmem_limit_bytes=24 * MIB),
        name="token",
    )(mine, other, w_atom_token, token_cond, gains, w_head)
    ring = groups // 2
    spread = []
    for by in STEPS:
        moves = []
        for low in range(2):
            for high in range(2):
                for z in range(ring):
                    for w in range(peers):
                        source = (high * ring + z) * size + low * peers + w
                        target = (low * ring + (z + by) % ring) * size + high * peers + w
                        moves.append((source, target))
        spread.append(lax.ppermute(kv, ("aa", "ba"), moves))

    mixed = pl.pallas_call(
        attend_kernel,
        out_shape=shape((peers, DUO + 16, tok_rows), BF),
        in_specs=whole(3 + ring),
        out_specs=whole(1)[0],
        compiler_params=pltpu.CompilerParams(vmem_limit_bytes=16 * MIB),
        cost_estimate=pl.CostEstimate(
            flops=20_000_000_000, bytes_accessed=8 * MIB, transcendentals=0
        ),
        name="attend",
    )(query, gate, bias, *spread)
    mine, other = gathered(mixed, same_core)

    return pl.pallas_call(
        close_kernel,
        out_shape=(shape((3, atoms), F32), shape((tok_rows, D), F32)),
        in_specs=whole(13),
        out_specs=tuple(whole(2)),
        compiler_params=pltpu.CompilerParams(vmem_limit_bytes=24 * MIB),
        name="close",
    )(
        mine, other, w_attn_out.reshape(peers // 2, 2, DUO, D), start, gains, w_up, w_down,
        w_token_atom, state, ids, w_pos_out, noisy_pos, noise,
    )


def solution(mesh):
    both = ("aa", "ba")
    in_specs = (
        P(both, None), P(None, both), P(), P(both), P("aa", None), P("aa", "ba", None),
        *[P()] * 11,
    )
    out_specs = (P(None, both), P("aa", None))
    return jax.shard_map(
        on_device, mesh=mesh, in_specs=in_specs, out_specs=out_specs, check_vma=False
    )
```
